32 devices in a mesh: clip: 16 (over z, y, core), seq: 2 (over x).
Axes of the slice: x: 2, y: 2, z: 4, core: 2. Of those that a mesh axis runs over, the one named last changes fastest.
Arguments:
- query_rows: bfloat16 [16, 384, 5120], P('clip', 'seq'), may hold values from -32 to 32
- key_rows: bfloat16 [16, 384, 5120], P('clip', 'seq'), may hold values from -32 to 32
- value_rows: bfloat16 [16, 384, 5120], P('clip', 'seq'), may hold values from -6 to 6
- query_gain: float32 [5120], replicated, may hold values from 0.1 to 1.9
- key_gain: float32 [5120], replicated, may hold values from 0.1 to 1.9
- tile_lists: int32 [16, 40, 3, 3], P(None, 'seq'), may hold values from 0 to 2, as said below
- tile_counts: int32 [16, 40, 3], P(None, 'seq'), may hold values from 1 to 3, as said below
Outputs:
- attended: bfloat16 [16, 384, 5120], P('clip', 'seq')
The draws below stay inside these ranges and needn't reach their ends.
Inputs may be any that keep to these rules, and one draw needn't show every extreme that they name: Each row tile_lists[c, h, b] is a permutation of 0 to 2 whose first entry is b; only its first tile_counts[c, h, b] entries are used. `tile_counts`: some entry equals 3 in every draw.
All inputs are finite; a program needn't handle non-finite values.
Results may differ from the reference program's by a relative error of at most 0.012.
The reference program's roundings to bfloat16 on the way count: a program that leaves them out, or rounds other values in their place, can miss the bound.
Values may be sent and summed in bfloat16 or wider, within the bound.
A program may use at most 128 MiB of HBM per device.

```python
import math
import jax
import jax.numpy as jnp
from jax import lax

H = 40
HD = 128
D = 5120
BLK = 128
L = 384
QB = 3
CLIPS = 16


def draw_query_rows(key, part):
    own_key = jax.random.fold_in(key, 7)
    return jnp.clip(jax.random.normal(own_key, (CLIPS, L, D), jnp.float32), -4.0, 4.0).astype(jnp.bfloat16)


def draw_key_rows(key, part):
    own_key = jax.random.fold_in(key, 9)
    return jnp.clip(jax.random.normal(own_key, (CLIPS, L, D), jnp.float32), -4.0, 4.0).astype(jnp.bfloat16)


def draw_tile_lists(key, part):
    key = jax.random.fold_in(key, 41)
    noise = jax.random.randint(key, (CLIPS, H, QB, QB), 0, 1 << 20, dtype=jnp.int32)
    blocks = jnp.arange(QB, dtype=jnp.int32)
    ordering = noise * QB + blocks
    ordering = jnp.where(blocks[:, None] == blocks[None, :], -1, ordering)
    return jnp.argsort(ordering, axis=-1, stable=True).astype(jnp.int32)


def draw_tile_counts(key, part):
    key = jax.random.fold_in(key, 31)
    level_key, count_key, spot_key = jax.random.split(key, 3)
    level = jax.random.randint(level_key, (CLIPS, 1, 1), 1, QB + 1, dtype=jnp.int32)
    counts = 1 + jax.random.randint(count_key, (CLIPS, H, QB), 0, level, dtype=jnp.int32)
    spot = jax.random.randint(spot_key, (3,), 0, jnp.array([CLIPS, H, QB], dtype=jnp.int32), dtype=jnp.int32)
    counts = counts.at[spot[0], spot[1], spot[2]].set(QB)
    return counts.astype(jnp.int32)


def block_levels(stream_key, extent, pieces, low, largest):
    level = 1.0
    for position, shards_of in pieces:
        draws = jax.random.uniform(jax.random.fold_in(jax.random.fold_in(stream_key, 6), position), (shards_of,), jnp.float32, low / len(pieces), largest / len(pieces))
        level = level * jnp.repeat(jnp.exp(draws), extent[position] // shards_of).reshape((-1,) + (1,) * (len(extent) - 1 - position))
    return level


def bell_draw(rng, dims, scale, most, shards=(), held_as=jnp.bfloat16):
    drawn = jax.random.normal(rng, dims, jnp.float32) * scale
    if len(shards) > 0:
        drawn = block_levels(rng, dims, shards, -0.22, 0.18) * drawn
    return jnp.clip(drawn, min=-most, max=most).astype(held_as)


def setup_inputs(seed: int = 0) -> dict:
    arg_keys = jax.random.split(jax.random.key(seed), 8)
    return {
        "query_rows": draw_query_rows(jax.random.fold_in(arg_keys[7], 71), 0),
        "key_rows": draw_key_rows(jax.random.fold_in(arg_keys[7], 71), 0),
        "value_rows": bell_draw(arg_keys[2], (CLIPS, L, D), 1.0, 6.0, ((0, 16), (1, 2))),
        "query_gain": jnp.clip(1.0 + 0.18 * jax.random.normal(arg_keys[3], (D,), jnp.float32), 0.1, 1.9),
        "key_gain": jnp.clip(1.0 + 0.18 * jax.random.normal(arg_keys[4], (D,), jnp.float32), 0.1, 1.9),
        "tile_lists": draw_tile_lists(jax.random.fold_in(arg_keys[7], 71), 0),
        "tile_counts": draw_tile_counts(jax.random.fold_in(arg_keys[7], 71), 0),
    }


epsilon = 1e-06

def rms_normed(rows, gain):
    values = rows.astype(jnp.float32)
    spread = lax.optimization_barrier(jnp.mean(values * values, axis=-1, keepdims=True))
    return (values * lax.rsqrt(spread + epsilon) * gain.astype(jnp.float32)).astype(jnp.bfloat16)

def block_allowed(tile_lists, tile_counts):
    blocks = jnp.arange(QB, dtype=jnp.int32)
    named_block = tile_lists[..., None] == blocks
    live_slot = blocks[:, None] < tile_counts[..., None, None]
    return jnp.any(named_block & live_slot, axis=-2)

def one_head(operands):
    query_head, key_head, value_head, allowed = operands
    scores = jnp.dot(query_head, key_head.T, preferred_element_type=jnp.float32)
    scores = scores * (1.0 / math.sqrt(HD))
    tile_mask = jnp.repeat(jnp.repeat(allowed, BLK, axis=0), BLK, axis=1)
    scores = jnp.where(tile_mask, scores, -jnp.inf)
    highest = lax.optimization_barrier(jnp.max(scores, axis=-1, keepdims=True))
    weights = jnp.exp(scores - highest)
    denominator = lax.optimization_barrier(jnp.sum(weights, axis=-1, keepdims=True))
    numerator = jnp.dot(weights.astype(jnp.bfloat16), value_head, preferred_element_type=jnp.float32)
    return (numerator / denominator).astype(jnp.bfloat16)

def heads_first(matrix):
    return matrix.reshape(L, H, HD).transpose(1, 0, 2)

def one_clip(operands):
    query_clip, key_clip, value_clip, allowed = operands
    outputs = lax.map(one_head, (heads_first(query_clip), heads_first(key_clip), heads_first(value_clip), allowed))
    return outputs.transpose(1, 0, 2).reshape(L, H * HD)

def reference(query_rows, key_rows, value_rows, query_gain, key_gain, tile_lists, tile_counts):
    query_normed = rms_normed(query_rows, query_gain)
    key_normed = rms_normed(key_rows, key_gain)
    allowed = block_allowed(tile_lists, tile_counts)
    return lax.map(one_clip, (query_normed, key_normed, value_rows, allowed))
```

```python
import functools
import math

import jax
import jax.numpy as jnp
from jax import lax
from jax.experimental import pallas as pl
from jax.experimental.pallas import tpu as pltpu
from jax.sharding import PartitionSpec as P

HD = 128
BLK = 128
PAIR = 2
AHEAD = 3
NORM_ROWS = 16
MASKED = -1e30
EPSILON = 1e-06

MESH = pl.DeviceIdType.MESH


def kernel(
    n,
    query_hbm,
    key_hbm,
    value_hbm,
    query_gain,
    key_gain,
    lists,
    counts,
    out_hbm,
    query_buf,
    key_buf,
    value_buf,
    out_buf,
    codes,
    codes_smem,
    load_sem,
    send_sem,
    recv_sem,
    code_send_sem,
    code_recv_sem,
    code_load_sem,
    out_sem,
):
    tokens, width = query_buf.shape
    head_count = width // HD
    own_heads = lists.shape[3]
    block_count = lists.shape[0]
    groups = head_count // PAIR
    group_width = PAIR * HD
    row_group = math.gcd(tokens, BLK)
    me = lax.axis_index("seq")
    clip = lax.axis_index("clip")

    def rows_of(device):
        return pl.ds(pl.multiple_of(device * tokens, row_group), tokens)

    def columns_of(group):
        return pl.ds(pl.multiple_of(group * group_width, group_width), group_width)

    key_load = pltpu.make_async_copy(key_hbm.at[0], key_buf.at[rows_of(me)], load_sem.at[0])
    query_load = pltpu.make_async_copy(query_hbm.at[0], query_buf, load_sem.at[1])
    value_load = pltpu.make_async_copy(value_hbm.at[0], value_buf.at[rows_of(me)], load_sem.at[2])
    key_load.start()
    query_load.start()
    value_load.start()

    barrier = pltpu.get_barrier_semaphore()
    for off in range(1, n):
        pl.semaphore_signal(
            barrier, inc=1, device_id={"seq": lax.rem(me + off, n)}, device_id_type=MESH
        )
    pl.semaphore_wait(barrier, n - 1)

    def value_send(off, group):
        place = (rows_of(me), columns_of(group))
        return pltpu.make_async_remote_copy(
            src_ref=value_hbm.at[0, :, columns_of(group)],
            dst_ref=value_buf.at[place],
            send_sem=send_sem.at[off - 1, 0, group],
            recv_sem=recv_sem.at[off - 1, 0, group],
            device_id={"seq": lax.rem(me + off, n)},
            device_id_type=MESH,
        )

    def key_send(off, group):
        place = (rows_of(me), columns_of(group))
        return pltpu.make_async_remote_copy(
            src_ref=key_buf.at[place],
            dst_ref=key_buf.at[place],
            send_sem=send_sem.at[off - 1, 1, group],
            recv_sem=recv_sem.at[off - 1, 1, group],
            device_id={"seq": lax.rem(me + off, n)},
            device_id_type=MESH,
        )

    def arrival(buf, kind, off, group):
        place = (rows_of(lax.rem(me + n - off, n)), columns_of(group))
        return pltpu.make_async_remote_copy(
            src_ref=buf.at[place],
            dst_ref=buf.at[place],
            send_sem=send_sem.at[off - 1, kind, group],
            recv_sem=recv_sem.at[off - 1, kind, group],
            device_id={"seq": lax.rem(me + off, n)},
            device_id_type=MESH,
        )

    for group in range(min(AHEAD, groups)):
        for off in range(1, n):
            value_send(off, group).start()

    codes[me] = jnp.zeros(codes.shape[1:], jnp.int32)
    for b in range(block_count):
        used = counts[b, pl.ds(clip, 1), :]
        code = jnp.zeros((1, own_heads), jnp.int32)
        for s in range(block_count):
            named = lists[b, s, pl.ds(clip, 1), :]
            for e in range(block_count):
                code = code + jnp.where((named == e) & (used > s), 1 << e, 0)
        codes[me, pl.ds(b, 1), pl.ds(0, own_heads)] = code

    def code_send(off):
        return pltpu.make_async_remote_copy(
            src_ref=codes.at[me],
            dst_ref=codes.at[me],
            send_sem=code_send_sem.at[off - 1],
            recv_sem=code_recv_sem.at[off - 1],
            device_id={"seq": lax.rem(me + off, n)},
            device_id_type=MESH,
        )

    for off in range(1, n):
        code_send(off).start()

    def normalise(buf, first, gain):
        def step(i, carry):
            rows = pl.ds(pl.multiple_of(first + i * NORM_ROWS, NORM_ROWS), NORM_ROWS)
            values = buf[rows, :].astype(jnp.float32)
            spread = jnp.sum(values * values, axis=-1, keepdims=True) * (1.0 / width)
            buf[rows, :] = (values * lax.rsqrt(spread + EPSILON) * gain[...]).astype(jnp.bfloat16)
            return carry

        lax.fori_loop(0, tokens // NORM_ROWS, step, 0)

    key_load.wait()
    normalise(key_buf, me * tokens, key_gain)
    for group in range(min(AHEAD, groups)):
        for off in range(1, n):
            key_send(off, group).start()
    query_load.wait()
    normalise(query_buf, 0, query_gain)
    value_load.wait()
    for off in range(1, n):
        source = lax.rem(me + n - off, n)
        pltpu.make_async_remote_copy(
            src_ref=codes.at[source],
            dst_ref=codes.at[source],
            send_sem=code_send_sem.at[off - 1],
            recv_sem=code_recv_sem.at[off - 1],
            device_id={"seq": lax.rem(me + off, n)},
            device_id_type=MESH,
        ).wait_recv()
    code_load = pltpu.make_async_copy(codes, codes_smem, code_load_sem)
    code_load.start()
    code_load.wait()

    exponent_scale = math.log2(math.e) / math.sqrt(HD)

    def attend(head):
        columns = pl.ds(pl.multiple_of(head * HD, HD), HD)
        scores = lax.dot_general(
            query_buf[:, columns],
            key_buf[:, columns],
            (((1,), (1,)), ((), ())),
            preferred_element_type=jnp.float32,
        )
        owner = head // own_heads
        own_head = head - owner * own_heads
        weights, sums = [], []
        for r in range(tokens // row_group):
            code = codes_smem[owner, (me * tokens + r * row_group) // BLK, own_head]
            pieces = []
            for e in range(block_count):
                allowed = jnp.bitwise_and(code, 1 << e) != 0
                bias = jnp.where(allowed, jnp.float32(0.0), jnp.float32(MASKED))
                pieces.append(
                    scores[r * row_group : (r + 1) * row_group, e * BLK : (e + 1) * BLK] + bias
                )
            masked = jnp.concatenate(pieces, axis=1)
            highest = jnp.max(masked, axis=-1, keepdims=True)
            weight = jnp.exp2((masked - highest) * exponent_scale)
            sums.append(jnp.sum(weight, axis=-1, keepdims=True))
            weights.append(weight.astype(jnp.bfloat16))
        numerator = jnp.dot(
            jnp.concatenate(weights, axis=0),
            value_buf[:, columns],
            preferred_element_type=jnp.float32,
        )
        out_buf[:, columns] = (numerator / jnp.concatenate(sums, axis=0)).astype(jnp.bfloat16)

    def out_copy(group):
        return pltpu.make_async_copy(
            out_buf.at[:, columns_of(group)], out_hbm.at[0, :, columns_of(group)], out_sem.at[group]
        )

    def visit(group, carry):
        for off in range(1, n):
            value_send(off, group).wait_send()
            key_send(off, group).wait_send()

        @pl.when(group + AHEAD < groups)
        def _():
            for off in range(1, n):
                value_send(off, group + AHEAD).start()
                key_send(off, group + AHEAD).start()

        for off in range(1, n):
            arrival(value_buf, 0, off, group).wait_recv()
            arrival(key_buf, 1, off, group).wait_recv()
        for j in range(PAIR):
            attend(group * PAIR + j)
        out_copy(group).start()
        return carry

    lax.fori_loop(0, groups, visit, 0)

    def finish(group, carry):
        out_copy(group).wait()
        return carry

    lax.fori_loop(0, groups, finish, 0)
    for off in range(1, n):
        code_send(off).wait_send()


def shards(n, query_rows, key_rows, value_rows, query_gain, key_gain, tile_lists, tile_counts):
    _, tokens, width = query_rows.shape
    block_count = tile_lists.shape[2]
    groups = width // (PAIR * HD)
    code_rows = -(-block_count // 8) * 8
    buffers = (2 * n + 2) * tokens * width * 2
    in_hbm = pl.BlockSpec(memory_space=pl.ANY)
    in_vmem = pl.BlockSpec(memory_space=pltpu.VMEM)
    visited = tokens * n * tokens * width
    return pl.pallas_call(
        functools.partial(kernel, n),
        out_shape=jax.ShapeDtypeStruct(query_rows.shape, jnp.bfloat16),
        in_specs=[in_hbm] * 3 + [in_vmem] * 4,
        out_specs=in_hbm,
        scratch_shapes=[
            pltpu.VMEM((tokens, width), jnp.bfloat16),
            pltpu.VMEM((n * tokens, width), jnp.bfloat16),
            pltpu.VMEM((n * tokens, width), jnp.bfloat16),
            pltpu.VMEM((tokens, width), jnp.bfloat16),
            pltpu.VMEM((n, code_rows, 128), jnp.int32),
            pltpu.SMEM((n, code_rows, 128), jnp.int32),
            pltpu.SemaphoreType.DMA((3,)),
            pltpu.SemaphoreType.DMA((n - 1, 2, groups)),
            pltpu.SemaphoreType.DMA((n - 1, 2, groups)),
            pltpu.SemaphoreType.DMA((n - 1,)),
            pltpu.SemaphoreType.DMA((n - 1,)),
            pltpu.SemaphoreType.DMA,
            pltpu.SemaphoreType.DMA((groups,)),
        ],
        compiler_params=pltpu.CompilerParams(
            collective_id=0,
            has_side_effects=True,
            vmem_limit_bytes=buffers + 12 * 1024 * 1024,
        ),
        cost_estimate=pl.CostEstimate(
            flops=4 * visited, bytes_accessed=8 * tokens * width, transcendentals=visited // HD
        ),
    )(
        query_rows,
        key_rows,
        value_rows,
        query_gain.reshape(1, width),
        key_gain.reshape(1, width),
        jnp.transpose(tile_lists, (2, 3, 0, 1)),
        jnp.transpose(tile_counts, (2, 0, 1)),
    )


def solution(mesh):
    in_specs = (
        P("clip", "seq", None),
        P("clip", "seq", None),
        P("clip", "seq", None),
        P(),
        P(),
        P(None, "seq", None, None),
        P(None, "seq", None),
    )
    out_specs = P("clip", "seq", None)
    return jax.shard_map(
        functools.partial(shards, mesh.shape["seq"]),
        mesh=mesh,
        in_specs=in_specs,
        out_specs=out_specs,
        check_vma=False,
    )
```

```python
import functools
import math

import jax
import jax.numpy as jnp
from jax import lax
from jax.experimental import pallas as pl
from jax.experimental.pallas import tpu as pltpu
from jax.sharding import PartitionSpec as P

HD = 128
BLK = 128
PAIR = 2
AHEAD = 3
NORM_ROWS = 16
MASKED = -1e30
VMEM_BYTES = 60 * 1024 * 1024
EPSILON = 1e-06

MESH = pl.DeviceIdType.MESH


def kernel(
    n,
    query_hbm,
    key_hbm,
    value_hbm,
    query_gain_hbm,
    key_gain_hbm,
    lists_hbm,
    counts_hbm,
    out_hbm,
    query_raw,
    key_raw,
    query_buf,
    key_buf,
    value_buf,
    out_buf,
    query_gain,
    key_gain,
    lists,
    counts,
    codes,
    codes_smem,
    load_sem,
    value_sem,
    send_sem,
    recv_sem,
    code_send_sem,
    code_recv_sem,
    code_load_sem,
    out_sem,
):
    tokens, width = query_raw.shape
    groups, _, group_width = key_buf.shape
    own_heads = lists.shape[3]
    block_count = lists.shape[0]
    row_group = math.gcd(tokens, BLK)
    first = min(AHEAD, groups)
    me = lax.axis_index("seq")
    clip = lax.axis_index("clip")

    def rows_of(device):
        return pl.ds(pl.multiple_of(device * tokens, row_group), tokens)

    def value_load(group):
        columns = pl.ds(pl.multiple_of(group * group_width, group_width), group_width)
        return pltpu.make_async_copy(
            value_hbm.at[0, :, columns], value_buf.at[group, rows_of(me)], value_sem.at[group]
        )

    loads = [
        pltpu.make_async_copy(source, target, load_sem.at[i])
        for i, (source, target) in enumerate(
            [
                (key_hbm.at[0], key_raw),
                (key_gain_hbm, key_gain),
                (lists_hbm, lists),
                (counts_hbm, counts),
                (query_hbm.at[0], query_raw),
                (query_gain_hbm, query_gain),
            ]
        )
    ]
    for group in range(first):
        value_load(group).start()
    for load in loads:
        load.start()

    barrier = pltpu.get_barrier_semaphore()
    for off in range(1, n):
        pl.semaphore_signal(
            barrier, inc=1, device_id={"seq": lax.rem(me + off, n)}, device_id_type=MESH
        )

    def load_values(group, carry):
        value_load(group).start()
        return carry

    lax.fori_loop(first, groups, load_values, 0)
    pl.semaphore_wait(barrier, n - 1)

    def message(buf, kind, off, group, source):
        place = (group, rows_of(source))
        return pltpu.make_async_remote_copy(
            src_ref=buf.at[place],
            dst_ref=buf.at[place],
            send_sem=send_sem.at[off - 1, kind, group],
            recv_sem=recv_sem.at[off - 1, kind, group],
            device_id={"seq": lax.rem(me + off, n)},
            device_id_type=MESH,
        )

    def value_send(off, group):
        return message(value_buf, 0, off, group, me)

    def key_send(off, group):
        return message(key_buf, 1, off, group, me)

    for group in range(first):
        value_load(group).wait()
        for off in range(1, n):
            value_send(off, group).start()

    def normalise(raw, gain, target, first_row):
        def step(i, carry):
            rows = pl.ds(pl.multiple_of(i * NORM_ROWS, NORM_ROWS), NORM_ROWS)
            rows_to = pl.ds(pl.multiple_of(first_row + i * NORM_ROWS, NORM_ROWS), NORM_ROWS)
            total = jnp.zeros((NORM_ROWS, group_width), jnp.float32)
            for g in range(groups):
                part = raw[rows, g * group_width : (g + 1) * group_width].astype(jnp.float32)
                total = total + part * part
            spread = jnp.sum(total, axis=-1, keepdims=True) * (1.0 / width)
            factor = lax.rsqrt(spread + EPSILON)
            for g in range(groups):
                columns = slice(g * group_width, (g + 1) * group_width)
                part = raw[rows, columns].astype(jnp.float32)
                target[g, rows_to, :] = (part * factor * gain[:, columns]).astype(jnp.bfloat16)
            return carry

        lax.fori_loop(0, tokens // NORM_ROWS, step, 0)

    loads[0].wait()
    loads[1].wait()
    normalise(key_raw, key_gain, key_buf, me * tokens)
    for group in range(first):
        for off in range(1, n):
            key_send(off, group).start()

    loads[2].wait()
    loads[3].wait()
    codes[me] = jnp.zeros(codes.shape[1:], jnp.int32)
    for b in range(block_count):
        used = counts[b, pl.ds(clip, 1), :]
        code = jnp.zeros((1, own_heads), jnp.int32)
        for s in range(block_count):
            named = lists[b, s, pl.ds(clip, 1), :]
            for e in range(block_count):
                code = code + jnp.where((named == e) & (used > s), 1 << e, 0)
        codes[me, pl.ds(b, 1), pl.ds(0, own_heads)] = code

    def code_message(off, source):
        return pltpu.make_async_remote_copy(
            src_ref=codes.at[source],
            dst_ref=codes.at[source],
            send_sem=code_send_sem.at[off - 1],
            recv_sem=code_recv_sem.at[off - 1],
            device_id={"seq": lax.rem(me + off, n)},
            device_id_type=MESH,
        )

    for off in range(1, n):
        code_message(off, me).start()
    loads[4].wait()
    loads[5].wait()
    normalise(query_raw, query_gain, query_buf, 0)
    for off in range(1, n):
        code_message(off, lax.rem(me + n - off, n)).wait_recv()
    code_load = pltpu.make_async_copy(codes, codes_smem, code_load_sem)
    code_load.start()
    code_load.wait()

    exponent_scale = math.log2(math.e) / math.sqrt(HD)

    def attend(group, j):
        head = group * PAIR + j
        columns = slice(j * HD, (j + 1) * HD)
        scores = lax.dot_general(
            query_buf[group, :, columns],
            key_buf[group, :, columns],
            (((1,), (1,)), ((), ())),
            preferred_element_type=jnp.float32,
        )
        owner = head // own_heads
        own_head = head - owner * own_heads
        weights, sums = [], []
        for r in range(tokens // row_group):
            code = codes_smem[owner, (me * tokens + r * row_group) // BLK, own_head]
            pieces = []
            for e in range(block_count):
                allowed = jnp.bitwise_and(code, 1 << e) != 0
                bias = jnp.where(allowed, jnp.float32(0.0), jnp.float32(MASKED))
                pieces.append(
                    scores[r * row_group : (r + 1) * row_group, e * BLK : (e + 1) * BLK] + bias
                )
            masked = jnp.concatenate(pieces, axis=1)
            highest = jnp.max(masked, axis=-1, keepdims=True)
            weight = jnp.exp2((masked - highest) * exponent_scale)
            sums.append(jnp.sum(weight, axis=-1, keepdims=True))
            weights.append(weight.astype(jnp.bfloat16))
        numerator = jnp.dot(
            jnp.concatenate(weights, axis=0),
            value_buf[group, :, columns],
            preferred_element_type=jnp.float32,
        )
        out_buf[:, pl.ds(pl.multiple_of(head * HD, HD), HD)] = (
            numerator / jnp.concatenate(sums, axis=0)
        ).astype(jnp.bfloat16)

    def out_copy(group):
        columns = pl.ds(pl.multiple_of(group * group_width, group_width), group_width)
        return pltpu.make_async_copy(
            out_buf.at[:, columns], out_hbm.at[0, :, columns], out_sem.at[group]
        )

    def visit(group, carry):
        for off in range(1, n):
            value_send(off, group).wait_send()
            key_send(off, group).wait_send()

        @pl.when(group + AHEAD < groups)
        def _():
            value_load(group + AHEAD).wait()
            for off in range(1, n):
                value_send(off, group + AHEAD).start()
                key_send(off, group + AHEAD).start()

        for off in range(1, n):
            source = lax.rem(me + n - off, n)
            message(value_buf, 0, off, group, source).wait_recv()
            message(key_buf, 1, off, group, source).wait_recv()
        for j in range(PAIR):
            attend(group, j)
        out_copy(group).start()
        return carry

    lax.fori_loop(0, groups, visit, 0)

    def finish(group, carry):
        out_copy(group).wait()
        return carry

    lax.fori_loop(0, groups, finish, 0)
    for off in range(1, n):
        code_message(off, me).wait_send()


def shards(n, query_rows, key_rows, value_rows, query_gain, key_gain, tile_lists, tile_counts):
    _, tokens, width = query_rows.shape
    lists = jnp.transpose(tile_lists, (2, 3, 0, 1))
    counts = jnp.transpose(tile_counts, (2, 0, 1))
    block_count = lists.shape[0]
    group_width = PAIR * HD
    groups = width // group_width
    code_rows = -(-block_count // 8) * 8
    visited = tokens * n * tokens * width
    return pl.pallas_call(
        functools.partial(kernel, n),
        out_shape=jax.ShapeDtypeStruct(query_rows.shape, jnp.bfloat16),
        in_specs=[pl.BlockSpec(memory_space=pltpu.HBM)] * 7,
        out_specs=pl.BlockSpec(memory_space=pltpu.HBM),
        scratch_shapes=[
            pltpu.VMEM((tokens, width), jnp.bfloat16),
            pltpu.VMEM((tokens, width), jnp.bfloat16),
            pltpu.VMEM((groups, tokens, group_width), jnp.bfloat16),
            pltpu.VMEM((groups, n * tokens, group_width), jnp.bfloat16),
            pltpu.VMEM((groups, n * tokens, group_width), jnp.bfloat16),
            pltpu.VMEM((tokens, width), jnp.bfloat16),
            pltpu.VMEM((1, width), jnp.float32),
            pltpu.VMEM((1, width), jnp.float32),
            pltpu.VMEM(lists.shape, jnp.int32),
            pltpu.VMEM(counts.shape, jnp.int32),
            pltpu.VMEM((n, code_rows, 128), jnp.int32),
            pltpu.SMEM((n, code_rows, 128), jnp.int32),
            pltpu.SemaphoreType.DMA((6,)),
            pltpu.SemaphoreType.DMA((groups,)),
            pltpu.SemaphoreType.DMA((n - 1, 2, groups)),
            pltpu.SemaphoreType.DMA((n - 1, 2, groups)),
            pltpu.SemaphoreType.DMA((n - 1,)),
            pltpu.SemaphoreType.DMA((n - 1,)),
            pltpu.SemaphoreType.DMA,
            pltpu.SemaphoreType.DMA((groups,)),
        ],
        compiler_params=pltpu.CompilerParams(
            collective_id=0,
            has_side_effects=True,
            vmem_limit_bytes=VMEM_BYTES,
        ),
        cost_estimate=pl.CostEstimate(
            flops=4 * visited, bytes_accessed=8 * tokens * width, transcendentals=visited // HD
        ),
    )(
        query_rows,
        key_rows,
        value_rows,
        query_gain.reshape(1, width),
        key_gain.reshape(1, width),
        lists,
        counts,
    )


def solution(mesh):
    in_specs = (
        P("clip", "seq", None),
        P("clip", "seq", None),
        P("clip", "seq", None),
        P(),
        P(),
        P(None, "seq", None, None),
        P(None, "seq", None),
    )
    out_specs = P("clip", "seq", None)
    return jax.shard_map(
        functools.partial(shards, mesh.shape["seq"]),
        mesh=mesh,
        in_specs=in_specs,
        out_specs=out_specs,
        check_vma=False,
    )
```

```python
import functools
import math

import jax
import jax.numpy as jnp
from jax import lax
from jax.experimental import pallas as pl
from jax.experimental.pallas import tpu as pltpu
from jax.sharding import PartitionSpec as P

HD = 128
BLK = 128
PAIR = 2
AHEAD = 3
NORM_ROWS = 16
MASKED = -1e30
VMEM_BYTES = 48 * 1024 * 1024
EPSILON = 1e-06

MESH = pl.DeviceIdType.MESH


def kernel(
    n,
    query_hbm,
    key_hbm,
    value_hbm,
    query_gain_hbm,
    key_gain_hbm,
    lists_hbm,
    counts_hbm,
    out_ref,
    query_raw,
    key_raw,
    query_buf,
    key_buf,
    value_buf,
    query_gain,
    key_gain,
    lists,
    counts,
    codes,
    codes_smem,
    load_sem,
    value_sem,
    send_sem,
    recv_sem,
    code_send_sem,
    code_recv_sem,
    code_load_sem,
):
    tokens, width = query_raw.shape
    groups, _, group_width = key_buf.shape
    own_heads = lists.shape[3]
    block_count = lists.shape[0]
    row_group = math.gcd(tokens, BLK)
    first = min(AHEAD, groups)
    me = lax.axis_index("seq")
    clip = lax.axis_index("clip")

    def rows_of(device):
        return pl.ds(pl.multiple_of(device * tokens, row_group), tokens)

    def value_load(group):
        columns = pl.ds(pl.multiple_of(group * group_width, group_width), group_width)
        return pltpu.make_async_copy(
            value_hbm.at[0, :, columns], value_buf.at[group, rows_of(me)], value_sem.at[group]
        )

    loads = [
        pltpu.make_async_copy(source, target, load_sem.at[i])
        for i, (source, target) in enumerate(
            [
                (key_hbm.at[0], key_raw),
                (key_gain_hbm, key_gain),
                (lists_hbm, lists),
                (counts_hbm, counts),
                (query_hbm.at[0], query_raw),
                (query_gain_hbm, query_gain),
            ]
        )
    ]
    for group in range(first):
        value_load(group).start()
    for load in loads:
        load.start()

    barrier = pltpu.get_barrier_semaphore()
    for off in range(1, n):
        pl.semaphore_signal(
            barrier, inc=1, device_id={"seq": lax.rem(me + off, n)}, device_id_type=MESH
        )

    def load_values(group, carry):
        value_load(group).start()
        return carry

    lax.fori_loop(first, groups, load_values, 0)
    pl.semaphore_wait(barrier, n - 1)

    def message(buf, kind, off, group, source):
        place = (group, rows_of(source))
        return pltpu.make_async_remote_copy(
            src_ref=buf.at[place],
            dst_ref=buf.at[place],
            send_sem=send_sem.at[off - 1, kind, group],
            recv_sem=recv_sem.at[off - 1, kind, group],
            device_id={"seq": lax.rem(me + off, n)},
            device_id_type=MESH,
        )

    def value_send(off, group):
        return message(value_buf, 0, off, group, me)

    def key_send(off, group):
        return message(key_buf, 1, off, group, me)

    for group in range(first):
        value_load(group).wait()
        for off in range(1, n):
            value_send(off, group).start()

    def normalise(raw, gain, target, first_row):
        def step(i, carry):
            rows = pl.ds(pl.multiple_of(i * NORM_ROWS, NORM_ROWS), NORM_ROWS)
            rows_to = pl.ds(pl.multiple_of(first_row + i * NORM_ROWS, NORM_ROWS), NORM_ROWS)
            total = jnp.zeros((NORM_ROWS, group_width), jnp.float32)
            for g in range(groups):
                part = raw[rows, g * group_width : (g + 1) * group_width].astype(jnp.float32)
                total = total + part * part
            spread = jnp.sum(total, axis=-1, keepdims=True) * (1.0 / width)
            factor = lax.rsqrt(spread + EPSILON)
            for g in range(groups):
                columns = slice(g * group_width, (g + 1) * group_width)
                part = raw[rows, columns].astype(jnp.float32)
                target[g, rows_to, :] = (part * factor * gain[:, columns]).astype(jnp.bfloat16)
            return carry

        lax.fori_loop(0, tokens // NORM_ROWS, step, 0)

    loads[0].wait()
    loads[1].wait()
    normalise(key_raw, key_gain, key_buf, me * tokens)
    for group in range(first):
        for off in range(1, n):
            key_send(off, group).start()

    loads[2].wait()
    loads[3].wait()
    codes[me] = jnp.zeros(codes.shape[1:], jnp.int32)
    for b in range(block_count):
        used = counts[b, pl.ds(clip, 1), :]
        code = jnp.zeros((1, own_heads), jnp.int32)
        for s in range(block_count):
            named = lists[b, s, pl.ds(clip, 1), :]
            for e in range(block_count):
                code = code + jnp.where((named == e) & (used > s), 1 << e, 0)
        codes[me, pl.ds(b, 1), pl.ds(0, own_heads)] = code

    def code_message(off, source):
        return pltpu.make_async_remote_copy(
            src_ref=codes.at[source],
            dst_ref=codes.at[source],
            send_sem=code_send_sem.at[off - 1],
            recv_sem=code_recv_sem.at[off - 1],
            device_id={"seq": lax.rem(me + off, n)},
            device_id_type=MESH,
        )

    for off in range(1, n):
        code_message(off, me).start()
    loads[4].wait()
    loads[5].wait()
    normalise(query_raw, query_gain, query_buf, 0)
    for off in range(1, n):
        code_message(off, lax.rem(me + n - off, n)).wait_recv()
    code_load = pltpu.make_async_copy(codes, codes_smem, code_load_sem)
    code_load.start()
    code_load.wait()

    exponent_scale = math.log2(math.e) / math.sqrt(HD)

    def weigh(group, j):
        head = group * PAIR + j
        columns = slice(j * HD, (j + 1) * HD)
        scores = lax.dot_general(
            query_buf[group, :, columns],
            key_buf[group, :, columns],
            (((1,), (1,)), ((), ())),
            preferred_element_type=jnp.float32,
        )
        owner = head // own_heads
        own_head = head - owner * own_heads
        weights, sums = [], []
        for r in range(tokens // row_group):
            code = codes_smem[owner, (me * tokens + r * row_group) // BLK, own_head]
            pieces = []
            for e in range(block_count):
                allowed = jnp.bitwise_and(code, 1 << e) != 0
                bias = jnp.where(allowed, jnp.float32(0.0), jnp.float32(MASKED))
                pieces.append(
                    scores[r * row_group : (r + 1) * row_group, e * BLK : (e + 1) * BLK] + bias
                )
            masked = jnp.concatenate(pieces, axis=1)
            highest = jnp.max(masked, axis=-1, keepdims=True)
            weight = jnp.exp2((masked - highest) * exponent_scale)
            sums.append(jnp.sum(weight, axis=-1, keepdims=True))
            weights.append(weight.astype(jnp.bfloat16))
        return jnp.concatenate(weights, axis=0), 1.0 / jnp.concatenate(sums, axis=0)

    def gather(group, j, weight, inverse):
        numerator = jnp.dot(
            weight,
            value_buf[group, :, j * HD : (j + 1) * HD],
            preferred_element_type=jnp.float32,
        )
        columns = pl.ds(pl.multiple_of((group * PAIR + j) * HD, HD), HD)
        out_ref[0, :, columns] = (numerator * inverse).astype(jnp.bfloat16)

    def visit(group, carry):
        for off in range(1, n):
            value_send(off, group).wait_send()
            key_send(off, group).wait_send()

        @pl.when(group + AHEAD < groups)
        def _():
            value_load(group + AHEAD).wait()
            for off in range(1, n):
                key_send(off, group + AHEAD).start()
            for off in range(1, n):
                value_send(off, group + AHEAD).start()

        sources = [(off, lax.rem(me + n - off, n)) for off in range(1, n)]
        for off, source in sources:
            message(key_buf, 1, off, group, source).wait_recv()
        weighed = [weigh(group, j) for j in range(PAIR)]
        for off, source in sources:
            message(value_buf, 0, off, group, source).wait_recv()
        for j in range(PAIR):
            gather(group, j, *weighed[j])
        return carry

    lax.fori_loop(0, groups, visit, 0)
    for off in range(1, n):
        code_message(off, me).wait_send()


def shards(n, query_rows, key_rows, value_rows, query_gain, key_gain, tile_lists, tile_counts):
    _, tokens, width = query_rows.shape
    lists = jnp.transpose(tile_lists, (2, 3, 0, 1))
    counts = jnp.transpose(tile_counts, (2, 0, 1))
    block_count = lists.shape[0]
    group_width = PAIR * HD
    groups = width // group_width
    code_rows = -(-block_count // 8) * 8
    visited = tokens * n * tokens * width
    return pl.pallas_call(
        functools.partial(kernel, n),
        out_shape=pltpu.VMEM(query_rows.shape, jnp.bfloat16),
        in_specs=[pl.BlockSpec(memory_space=pltpu.HBM)] * 7,
        out_specs=pl.BlockSpec(memory_space=pltpu.VMEM),
        scratch_shapes=[
            pltpu.VMEM((tokens, width), jnp.bfloat16),
            pltpu.VMEM((tokens, width), jnp.bfloat16),
            pltpu.VMEM((groups, tokens, group_width), jnp.bfloat16),
            pltpu.VMEM((groups, n * tokens, group_width), jnp.bfloat16),
            pltpu.VMEM((groups, n * tokens, group_width), jnp.bfloat16),
            pltpu.VMEM((1, width), jnp.float32),
            pltpu.VMEM((1, width), jnp.float32),
            pltpu.VMEM(lists.shape, jnp.int32),
            pltpu.VMEM(counts.shape, jnp.int32),
            pltpu.VMEM((n, code_rows, 128), jnp.int32),
            pltpu.SMEM((n, code_rows, 128), jnp.int32),
            pltpu.SemaphoreType.DMA((6,)),
            pltpu.SemaphoreType.DMA((groups,)),
            pltpu.SemaphoreType.DMA((n - 1, 2, groups)),
            pltpu.SemaphoreType.DMA((n - 1, 2, groups)),
            pltpu.SemaphoreType.DMA((n - 1,)),
            pltpu.SemaphoreType.DMA((n - 1,)),
            pltpu.SemaphoreType.DMA,
        ],
        compiler_params=pltpu.CompilerParams(
            collective_id=0,
            has_side_effects=True,
            vmem_limit_bytes=VMEM_BYTES,
        ),
        cost_estimate=pl.CostEstimate(
            flops=4 * visited, bytes_accessed=8 * tokens * width, transcendentals=visited // HD
        ),
    )(
        *(
            pltpu.with_memory_space_constraint(operand, pltpu.HBM)
            for operand in (
                query_rows,
                key_rows,
                value_rows,
                query_gain.reshape(1, width),
                key_gain.reshape(1, width),
                lists,
                counts,
            )
        )
    )


def solution(mesh):
    in_specs = (
        P("clip", "seq", None),
        P("clip", "seq", None),
        P("clip", "seq", None),
        P(),
        P(),
        P(None, "seq", None, None),
        P(None, "seq", None),
    )
    out_specs = P("clip", "seq", None)
    return jax.shard_map(
        functools.partial(shards, mesh.shape["seq"]),
        mesh=mesh,
        in_specs=in_specs,
        out_specs=out_specs,
        check_vma=False,
    )
```

```python
import functools
import math

import jax
import jax.numpy as jnp
from jax import lax
from jax.experimental import pallas as pl
from jax.experimental.pallas import tpu as pltpu
from jax.sharding import PartitionSpec as P

HD = 128
BLK = 128
PAIR = 2
AHEAD = 8
NORM_ROWS = 16
MASKED = -1e30
VMEM_BYTES = 48 * 1024 * 1024
EPSILON = 1e-06

MESH = pl.DeviceIdType.MESH


def kernel(
    n,
    query_hbm,
    key_hbm,
    value_hbm,
    query_gain_hbm,
    key_gain_hbm,
    lists_hbm,
    counts_hbm,
    out_ref,
    query_raw,
    key_raw,
    query_buf,
    key_buf,
    value_buf,
    query_gain,
    key_gain,
    lists,
    counts,
    codes,
    codes_smem,
    load_sem,
    value_sem,
    send_sem,
    recv_sem,
    code_send_sem,
    code_recv_sem,
    code_load_sem,
):
    tokens, width = query_raw.shape
    groups, _, group_width = key_buf.shape
    own_heads = lists.shape[3]
    block_count = lists.shape[0]
    row_group = math.gcd(tokens, BLK)
    first = min(AHEAD, groups)
    me = lax.axis_index("seq")
    clip = lax.axis_index("clip")

    def rows_of(device):
        return pl.ds(pl.multiple_of(device * tokens, row_group), tokens)

    def value_load(group):
        columns = pl.ds(pl.multiple_of(group * group_width, group_width), group_width)
        return pltpu.make_async_copy(
            value_hbm.at[0, :, columns], value_buf.at[group, rows_of(me)], value_sem.at[group]
        )

    loads = [
        pltpu.make_async_copy(source, target, load_sem.at[i])
        for i, (source, target) in enumerate(
            [
                (key_hbm.at[0], key_raw),
                (key_gain_hbm, key_gain),
                (lists_hbm, lists),
                (counts_hbm, counts),
                (query_hbm.at[0], query_raw),
                (query_gain_hbm, query_gain),
            ]
        )
    ]
    for group in range(first):
        value_load(group).start()
    for load in loads:
        load.start()

    barrier = pltpu.get_barrier_semaphore()
    for off in range(1, n):
        pl.semaphore_signal(
            barrier, inc=1, device_id={"seq": lax.rem(me + off, n)}, device_id_type=MESH
        )

    def load_values(group, carry):
        value_load(group).start()
        return carry

    lax.fori_loop(first, groups, load_values, 0)
    pl.semaphore_wait(barrier, n - 1)

    def message(buf, kind, off, group, source):
        place = (group, rows_of(source))
        return pltpu.make_async_remote_copy(
            src_ref=buf.at[place],
            dst_ref=buf.at[place],
            send_sem=send_sem.at[off - 1, kind, group],
            recv_sem=recv_sem.at[off - 1, kind, group],
            device_id={"seq": lax.rem(me + off, n)},
            device_id_type=MESH,
        )

    def value_send(off, group):
        return message(value_buf, 0, off, group, me)

    def key_send(off, group):
        return message(key_buf, 1, off, group, me)

    for group in range(first):
        value_load(group).wait()
        for off in range(1, n):
            value_send(off, group).start()

    def normalise(raw, gain, target, first_row):
        def step(i, carry):
            rows = pl.ds(pl.multiple_of(i * NORM_ROWS, NORM_ROWS), NORM_ROWS)
            rows_to = pl.ds(pl.multiple_of(first_row + i * NORM_ROWS, NORM_ROWS), NORM_ROWS)
            total = jnp.zeros((NORM_ROWS, group_width), jnp.float32)
            for g in range(groups):
                part = raw[rows, g * group_width : (g + 1) * group_width].astype(jnp.float32)
                total = total + part * part
            spread = jnp.sum(total, axis=-1, keepdims=True) * (1.0 / width)
            factor = lax.rsqrt(spread + EPSILON)
            for g in range(groups):
                columns = slice(g * group_width, (g + 1) * group_width)
                part = raw[rows, columns].astype(jnp.float32)
                target[g, rows_to, :] = (part * factor * gain[:, columns]).astype(jnp.bfloat16)
            return carry

        lax.fori_loop(0, tokens // NORM_ROWS, step, 0)

    loads[0].wait()
    loads[1].wait()
    normalise(key_raw, key_gain, key_buf, me * tokens)
    for group in range(first):
        for off in range(1, n):
            key_send(off, group).start()

    loads[2].wait()
    loads[3].wait()
    codes[me] = jnp.zeros(codes.shape[1:], jnp.int32)
    for b in range(block_count):
        used = counts[b, pl.ds(clip, 1), :]
        code = jnp.zeros((1, own_heads), jnp.int32)
        for s in range(block_count):
            named = lists[b, s, pl.ds(clip, 1), :]
            for e in range(block_count):
                code = code + jnp.where((named == e) & (used > s), 1 << e, 0)
        codes[me, pl.ds(b, 1), pl.ds(0, own_heads)] = code

    def code_message(off, source):
        return pltpu.make_async_remote_copy(
            src_ref=codes.at[source],
            dst_ref=codes.at[source],
            send_sem=code_send_sem.at[off - 1],
            recv_sem=code_recv_sem.at[off - 1],
            device_id={"seq": lax.rem(me + off, n)},
            device_id_type=MESH,
        )

    for off in range(1, n):
        code_message(off, me).start()
    loads[4].wait()
    loads[5].wait()
    normalise(query_raw, query_gain, query_buf, 0)
    for off in range(1, n):
        code_message(off, lax.rem(me + n - off, n)).wait_recv()
    code_load = pltpu.make_async_copy(codes, codes_smem, code_load_sem)
    code_load.start()
    code_load.wait()

    exponent_scale = math.log2(math.e) / math.sqrt(HD)

    def weigh(group, j):
        head = group * PAIR + j
        columns = slice(j * HD, (j + 1) * HD)
        scores = lax.dot_general(
            query_buf[group, :, columns],
            key_buf[group, :, columns],
            (((1,), (1,)), ((), ())),
            preferred_element_type=jnp.float32,
        )
        owner = head // own_heads
        own_head = head - owner * own_heads
        weights, sums = [], []
        for r in range(tokens // row_group):
            code = codes_smem[owner, (me * tokens + r * row_group) // BLK, own_head]
            pieces = []
            for e in range(block_count):
                allowed = jnp.bitwise_and(code, 1 << e) != 0
                bias = jnp.where(allowed, jnp.float32(0.0), jnp.float32(MASKED))
                pieces.append(
                    scores[r * row_group : (r + 1) * row_group, e * BLK : (e + 1) * BLK] + bias
                )
            masked = jnp.concatenate(pieces, axis=1)
            highest = jnp.max(masked, axis=-1, keepdims=True)
            weight = jnp.exp2((masked - highest) * exponent_scale)
            sums.append(jnp.sum(weight, axis=-1, keepdims=True))
            weights.append(weight.astype(jnp.bfloat16))
        return jnp.concatenate(weights, axis=0), 1.0 / jnp.concatenate(sums, axis=0)

    def gather(group, j, weight, inverse):
        numerator = jnp.dot(
            weight,
            value_buf[group, :, j * HD : (j + 1) * HD],
            preferred_element_type=jnp.float32,
        )
        columns = pl.ds(pl.multiple_of((group * PAIR + j) * HD, HD), HD)
        out_ref[0, :, columns] = (numerator * inverse).astype(jnp.bfloat16)

    def visit(group, carry):
        for off in range(1, n):
            value_send(off, group).wait_send()
            key_send(off, group).wait_send()

        @pl.when(group + AHEAD < groups)
        def _():
            value_load(group + AHEAD).wait()
            for off in range(1, n):
                key_send(off, group + AHEAD).start()
            for off in range(1, n):
                value_send(off, group + AHEAD).start()

        sources = [(off, lax.rem(me + n - off, n)) for off in range(1, n)]
        for off, source in sources:
            message(key_buf, 1, off, group, source).wait_recv()
        weighed = [weigh(group, j) for j in range(PAIR)]
        for off, source in sources:
            message(value_buf, 0, off, group, source).wait_recv()
        for j in range(PAIR):
            gather(group, j, *weighed[j])
        return carry

    lax.fori_loop(0, groups, visit, 0)
    for off in range(1, n):
        code_message(off, me).wait_send()


def shards(n, query_rows, key_rows, value_rows, query_gain, key_gain, tile_lists, tile_counts):
    _, tokens, width = query_rows.shape
    lists = jnp.transpose(tile_lists, (2, 3, 0, 1))
    counts = jnp.transpose(tile_counts, (2, 0, 1))
    block_count = lists.shape[0]
    group_width = PAIR * HD
    groups = width // group_width
    code_rows = -(-block_count // 8) * 8
    visited = tokens * n * tokens * width
    return pl.pallas_call(
        functools.partial(kernel, n),
        out_shape=pltpu.VMEM(query_rows.shape, jnp.bfloat16),
        in_specs=[pl.BlockSpec(memory_space=pltpu.HBM)] * 7,
        out_specs=pl.BlockSpec(memory_space=pltpu.VMEM),
        scratch_shapes=[
            pltpu.VMEM((tokens, width), jnp.bfloat16),
            pltpu.VMEM((tokens, width), jnp.bfloat16),
            pltpu.VMEM((groups, tokens, group_width), jnp.bfloat16),
            pltpu.VMEM((groups, n * tokens, group_width), jnp.bfloat16),
            pltpu.VMEM((groups, n * tokens, group_width), jnp.bfloat16),
            pltpu.VMEM((1, width), jnp.float32),
            pltpu.VMEM((1, width), jnp.float32),
            pltpu.VMEM(lists.shape, jnp.int32),
            pltpu.VMEM(counts.shape, jnp.int32),
            pltpu.VMEM((n, code_rows, 128), jnp.int32),
            pltpu.SMEM((n, code_rows, 128), jnp.int32),
            pltpu.SemaphoreType.DMA((6,)),
            pltpu.SemaphoreType.DMA((groups,)),
            pltpu.SemaphoreType.DMA((n - 1, 2, groups)),
            pltpu.SemaphoreType.DMA((n - 1, 2, groups)),
            pltpu.SemaphoreType.DMA((n - 1,)),
            pltpu.SemaphoreType.DMA((n - 1,)),
            pltpu.SemaphoreType.DMA,
        ],
        compiler_params=pltpu.CompilerParams(
            collective_id=0,
            has_side_effects=True,
            vmem_limit_bytes=VMEM_BYTES,
        ),
        cost_estimate=pl.CostEstimate(
            flops=4 * visited, bytes_accessed=8 * tokens * width, transcendentals=visited // HD
        ),
    )(
        *(
            pltpu.with_memory_space_constraint(operand, pltpu.HBM)
            for operand in (
                query_rows,
                key_rows,
                value_rows,
                query_gain.reshape(1, width),
                key_gain.reshape(1, width),
                lists,
                counts,
            )
        )
    )


def solution(mesh):
    in_specs = (
        P("clip", "seq", None),
        P("clip", "seq", None),
        P("clip", "seq", None),
        P(),
        P(),
        P(None, "seq", None, None),
        P(None, "seq", None),
    )
    out_specs = P("clip", "seq", None)
    return jax.shard_map(
        functools.partial(shards, mesh.shape["seq"]),
        mesh=mesh,
        in_specs=in_specs,
        out_specs=out_specs,
        check_vma=False,
    )
```

```python
import functools
import math

import jax
import jax.numpy as jnp
from jax import lax
from jax.experimental import pallas as pl
from jax.experimental.pallas import tpu as pltpu
from jax.sharding import PartitionSpec as P

HD = 128
BLK = 128
PAIR = 2
AHEAD = 4
NORM_ROWS = 16
MASKED = -1e30
VMEM_BYTES = 48 * 1024 * 1024
EPSILON = 1e-06

MESH = pl.DeviceIdType.MESH


def kernel(
    n,
    query_hbm,
    key_hbm,
    value_hbm,
    query_gain_hbm,
    key_gain_hbm,
    lists_hbm,
    counts_hbm,
    out_ref,
    query_raw,
    key_raw,
    query_buf,
    key_buf,
    value_buf,
    query_gain,
    key_gain,
    lists,
    counts,
    codes,
    codes_smem,
    load_sem,
    value_sem,
    send_sem,
    recv_sem,
    code_send_sem,
    code_recv_sem,
    code_load_sem,
):
    tokens, width = query_raw.shape
    groups, _, group_width = key_buf.shape
    own_heads = lists.shape[3]
    block_count = lists.shape[0]
    row_group = math.gcd(tokens, BLK)
    first = min(AHEAD, groups)
    me = lax.axis_index("seq")
    clip = lax.axis_index("clip")

    def rows_of(device):
        return pl.ds(pl.multiple_of(device * tokens, row_group), tokens)

    def value_load(group):
        columns = pl.ds(pl.multiple_of(group * group_width, group_width), group_width)
        return pltpu.make_async_copy(
            value_hbm.at[0, :, columns], value_buf.at[group, rows_of(me)], value_sem.at[group]
        )

    loads = [
        pltpu.make_async_copy(source, target, load_sem.at[i])
        for i, (source, target) in enumerate(
            [
                (key_hbm.at[0], key_raw),
                (key_gain_hbm, key_gain),
                (lists_hbm, lists),
                (counts_hbm, counts),
                (query_hbm.at[0], query_raw),
                (query_gain_hbm, query_gain),
            ]
        )
    ]
    barrier = pltpu.get_barrier_semaphore()
    for off in range(1, n):
        pl.semaphore_signal(
            barrier, inc=1, device_id={"seq": lax.rem(me + off, n)}, device_id_type=MESH
        )
    for load in loads:
        load.start()
    pl.semaphore_wait(barrier, n - 1)

    def message(buf, kind, off, group, source):
        place = (group, rows_of(source))
        return pltpu.make_async_remote_copy(
            src_ref=buf.at[place],
            dst_ref=buf.at[place],
            send_sem=send_sem.at[off - 1, kind, group],
            recv_sem=recv_sem.at[off - 1, kind, group],
            device_id={"seq": lax.rem(me + off, n)},
            device_id_type=MESH,
        )

    def value_send(off, group):
        columns = pl.ds(pl.multiple_of(group * group_width, group_width), group_width)
        return pltpu.make_async_remote_copy(
            src_ref=value_hbm.at[0, :, columns],
            dst_ref=value_buf.at[group, rows_of(me)],
            send_sem=send_sem.at[off - 1, 0, group],
            recv_sem=recv_sem.at[off - 1, 0, group],
            device_id={"seq": lax.rem(me + off, n)},
            device_id_type=MESH,
        )

    def key_send(off, group):
        return message(key_buf, 1, off, group, me)

    for group in range(first):
        for off in range(1, n):
            value_send(off, group).start()

    def load_values(group, carry):
        value_load(group).start()
        return carry

    lax.fori_loop(0, groups, load_values, 0)

    def normalise(raw, gain, target, first_row):
        def step(i, carry):
            rows = pl.ds(pl.multiple_of(i * NORM_ROWS, NORM_ROWS), NORM_ROWS)
            rows_to = pl.ds(pl.multiple_of(first_row + i * NORM_ROWS, NORM_ROWS), NORM_ROWS)
            total = jnp.zeros((NORM_ROWS, group_width), jnp.float32)
            for g in range(groups):
                part = raw[rows, g * group_width : (g + 1) * group_width].astype(jnp.float32)
                total = total + part * part
            spread = jnp.sum(total, axis=-1, keepdims=True) * (1.0 / width)
            factor = lax.rsqrt(spread + EPSILON)
            for g in range(groups):
                columns = slice(g * group_width, (g + 1) * group_width)
                part = raw[rows, columns].astype(jnp.float32)
                target[g, rows_to, :] = (part * factor * gain[:, columns]).astype(jnp.bfloat16)
            return carry

        lax.fori_loop(0, tokens // NORM_ROWS, step, 0)

    loads[0].wait()
    loads[1].wait()
    normalise(key_raw, key_gain, key_buf, me * tokens)
    for group in range(first):
        for off in range(1, n):
            key_send(off, group).start()

    loads[2].wait()
    loads[3].wait()
    codes[me] = jnp.zeros(codes.shape[1:], jnp.int32)
    for b in range(block_count):
        used = counts[b, pl.ds(clip, 1), :]
        code = jnp.zeros((1, own_heads), jnp.int32)
        for s in range(block_count):
            named = lists[b, s, pl.ds(clip, 1), :]
            for e in range(block_count):
                code = code + jnp.where((named == e) & (used > s), 1 << e, 0)
        codes[me, pl.ds(b, 1), pl.ds(0, own_heads)] = code

    def code_message(off, source):
        return pltpu.make_async_remote_copy(
            src_ref=codes.at[source],
            dst_ref=codes.at[source],
            send_sem=code_send_sem.at[off - 1],
            recv_sem=code_recv_sem.at[off - 1],
            device_id={"seq": lax.rem(me + off, n)},
            device_id_type=MESH,
        )

    for off in range(1, n):
        code_message(off, me).start()
    loads[4].wait()
    loads[5].wait()
    normalise(query_raw, query_gain, query_buf, 0)
    for off in range(1, n):
        code_message(off, lax.rem(me + n - off, n)).wait_recv()
    code_load = pltpu.make_async_copy(codes, codes_smem, code_load_sem)
    code_load.start()
    code_load.wait()

    exponent_scale = math.log2(math.e) / math.sqrt(HD)

    def weigh(group, j):
        head = group * PAIR + j
        columns = slice(j * HD, (j + 1) * HD)
        scores = lax.dot_general(
            query_buf[group, :, columns],
            key_buf[group, :, columns],
            (((1,), (1,)), ((), ())),
            preferred_element_type=jnp.float32,
        )
        owner = head // own_heads
        own_head = head - owner * own_heads
        weights, sums = [], []
        for r in range(tokens // row_group):
            code = codes_smem[owner, (me * tokens + r * row_group) // BLK, own_head]
            pieces = []
            for e in range(block_count):
                allowed = jnp.bitwise_and(code, 1 << e) != 0
                bias = jnp.where(allowed, jnp.float32(0.0), jnp.float32(MASKED))
                pieces.append(
                    scores[r * row_group : (r + 1) * row_group, e * BLK : (e + 1) * BLK] + bias
                )
            masked = jnp.concatenate(pieces, axis=1)
            highest = jnp.max(masked, axis=-1, keepdims=True)
            weight = jnp.exp2((masked - highest) * exponent_scale)
            sums.append(jnp.sum(weight, axis=-1, keepdims=True))
            weights.append(weight.astype(jnp.bfloat16))
        return jnp.concatenate(weights, axis=0), 1.0 / jnp.concatenate(sums, axis=0)

    def gather(group, j, weight, inverse):
        numerator = jnp.dot(
            weight,
            value_buf[group, :, j * HD : (j + 1) * HD],
            preferred_element_type=jnp.float32,
        )
        columns = pl.ds(pl.multiple_of((group * PAIR + j) * HD, HD), HD)
        out_ref[0, :, columns] = (numerator * inverse).astype(jnp.bfloat16)

    def visit(group, carry):
        for off in range(1, n):
            value_send(off, group).wait_send()
            key_send(off, group).wait_send()

        @pl.when(group + AHEAD < groups)
        def _():
            for off in range(1, n):
                key_send(off, group + AHEAD).start()
            for off in range(1, n):
                value_send(off, group + AHEAD).start()

        sources = [(off, lax.rem(me + n - off, n)) for off in range(1, n)]
        for off, source in sources:
            message(key_buf, 1, off, group, source).wait_recv()
        weighed = [weigh(group, j) for j in range(PAIR)]
        value_load(group).wait()
        for off, source in sources:
            message(value_buf, 0, off, group, source).wait_recv()
        for j in range(PAIR):
            gather(group, j, *weighed[j])
        return carry

    lax.fori_loop(0, groups, visit, 0)
    for off in range(1, n):
        code_message(off, me).wait_send()


def shards(n, query_rows, key_rows, value_rows, query_gain, key_gain, tile_lists, tile_counts):
    _, tokens, width = query_rows.shape
    lists = jnp.transpose(tile_lists, (2, 3, 0, 1))
    counts = jnp.transpose(tile_counts, (2, 0, 1))
    block_count = lists.shape[0]
    group_width = PAIR * HD
    groups = width // group_width
    code_rows = -(-block_count // 8) * 8
    visited = tokens * n * tokens * width
    return pl.pallas_call(
        functools.partial(kernel, n),
        out_shape=pltpu.VMEM(query_rows.shape, jnp.bfloat16),
        in_specs=[pl.BlockSpec(memory_space=pltpu.HBM)] * 7,
        out_specs=pl.BlockSpec(memory_space=pltpu.VMEM),
        scratch_shapes=[
            pltpu.VMEM((tokens, width), jnp.bfloat16),
            pltpu.VMEM((tokens, width), jnp.bfloat16),
            pltpu.VMEM((groups, tokens, group_width), jnp.bfloat16),
            pltpu.VMEM((groups, n * tokens, group_width), jnp.bfloat16),
            pltpu.VMEM((groups, n * tokens, group_width), jnp.bfloat16),
            pltpu.VMEM((1, width), jnp.float32),
            pltpu.VMEM((1, width), jnp.float32),
            pltpu.VMEM(lists.shape, jnp.int32),
            pltpu.VMEM(counts.shape, jnp.int32),
            pltpu.VMEM((n, code_rows, 128), jnp.int32),
            pltpu.SMEM((n, code_rows, 128), jnp.int32),
            pltpu.SemaphoreType.DMA((6,)),
            pltpu.SemaphoreType.DMA((groups,)),
            pltpu.SemaphoreType.DMA((n - 1, 2, groups)),
            pltpu.SemaphoreType.DMA((n - 1, 2, groups)),
            pltpu.SemaphoreType.DMA((n - 1,)),
            pltpu.SemaphoreType.DMA((n - 1,)),
            pltpu.SemaphoreType.DMA,
        ],
        compiler_params=pltpu.CompilerParams(
            collective_id=0,
            has_side_effects=True,
            vmem_limit_bytes=VMEM_BYTES,
        ),
        cost_estimate=pl.CostEstimate(
            flops=4 * visited, bytes_accessed=8 * tokens * width, transcendentals=visited // HD
        ),
    )(
        *(
            pltpu.with_memory_space_constraint(operand, pltpu.HBM)
            for operand in (
                query_rows,
                key_rows,
                value_rows,
                query_gain.reshape(1, width),
                key_gain.reshape(1, width),
                lists,
                counts,
            )
        )
    )


def solution(mesh):
    in_specs = (
        P("clip", "seq", None),
        P("clip", "seq", None),
        P("clip", "seq", None),
        P(),
        P(),
        P(None, "seq", None, None),
        P(None, "seq", None),
    )
    out_specs = P("clip", "seq", None)
    return jax.shard_map(
        functools.partial(shards, mesh.shape["seq"]),
        mesh=mesh,
        in_specs=in_specs,
        out_specs=out_specs,
        check_vma=False,
    )
```

```python
import functools
import math

import jax
import jax.numpy as jnp
from jax import lax
from jax.experimental import pallas as pl
from jax.experimental.pallas import tpu as pltpu
from jax.sharding import PartitionSpec as P

HD = 128
BLK = 128
PAIR = 4
AHEAD = 3
NORM_ROWS = 16
MASKED = -1e30
VMEM_BYTES = 48 * 1024 * 1024
EPSILON = 1e-06

MESH = pl.DeviceIdType.MESH


def kernel(
    n,
    query_hbm,
    key_hbm,
    value_hbm,
    query_gain_hbm,
    key_gain_hbm,
    lists_hbm,
    counts_hbm,
    out_ref,
    query_raw,
    key_raw,
    query_buf,
    key_buf,
    value_buf,
    query_gain,
    key_gain,
    lists,
    counts,
    codes,
    codes_smem,
    load_sem,
    value_sem,
    send_sem,
    recv_sem,
    code_send_sem,
    code_recv_sem,
    code_load_sem,
):
    tokens, width = query_raw.shape
    groups, _, group_width = key_buf.shape
    own_heads = lists.shape[3]
    block_count = lists.shape[0]
    row_group = math.gcd(tokens, BLK)
    first = min(AHEAD, groups)
    me = lax.axis_index("seq")
    clip = lax.axis_index("clip")

    def rows_of(device):
        return pl.ds(pl.multiple_of(device * tokens, row_group), tokens)

    def value_load(group):
        columns = pl.ds(pl.multiple_of(group * group_width, group_width), group_width)
        return pltpu.make_async_copy(
            value_hbm.at[0, :, columns], value_buf.at[group, rows_of(me)], value_sem.at[group]
        )

    loads = [
        pltpu.make_async_copy(source, target, load_sem.at[i])
        for i, (source, target) in enumerate(
            [
                (key_hbm.at[0], key_raw),
                (key_gain_hbm, key_gain),
                (lists_hbm, lists),
                (counts_hbm, counts),
                (query_hbm.at[0], query_raw),
                (query_gain_hbm, query_gain),
            ]
        )
    ]
    barrier = pltpu.get_barrier_semaphore()
    for off in range(1, n):
        pl.semaphore_signal(
            barrier, inc=1, device_id={"seq": lax.rem(me + off, n)}, device_id_type=MESH
        )
    for load in loads:
        load.start()
    pl.semaphore_wait(barrier, n - 1)

    def message(buf, kind, off, group, source):
        place = (group, rows_of(source))
        return pltpu.make_async_remote_copy(
            src_ref=buf.at[place],
            dst_ref=buf.at[place],
            send_sem=send_sem.at[off - 1, kind, group],
            recv_sem=recv_sem.at[off - 1, kind, group],
            device_id={"seq": lax.rem(me + off, n)},
            device_id_type=MESH,
        )

    def value_send(off, group):
        columns = pl.ds(pl.multiple_of(group * group_width, group_width), group_width)
        return pltpu.make_async_remote_copy(
            src_ref=value_hbm.at[0, :, columns],
            dst_ref=value_buf.at[group, rows_of(me)],
            send_sem=send_sem.at[off - 1, 0, group],
            recv_sem=recv_sem.at[off - 1, 0, group],
            device_id={"seq": lax.rem(me + off, n)},
            device_id_type=MESH,
        )

    def key_send(off, group):
        return message(key_buf, 1, off, group, me)

    for group in range(first):
        for off in range(1, n):
            value_send(off, group).start()

    def load_values(group, carry):
        value_load(group).start()
        return carry

    lax.fori_loop(0, groups, load_values, 0)

    def normalise(raw, gain, target, first_row):
        def step(i, carry):
            rows = pl.ds(pl.multiple_of(i * NORM_ROWS, NORM_ROWS), NORM_ROWS)
            rows_to = pl.ds(pl.multiple_of(first_row + i * NORM_ROWS, NORM_ROWS), NORM_ROWS)
            total = jnp.zeros((NORM_ROWS, group_width), jnp.float32)
            for g in range(groups):
                part = raw[rows, g * group_width : (g + 1) * group_width].astype(jnp.float32)
                total = total + part * part
            spread = jnp.sum(total, axis=-1, keepdims=True) * (1.0 / width)
            factor = lax.rsqrt(spread + EPSILON)
            for g in range(groups):
                columns = slice(g * group_width, (g + 1) * group_width)
                part = raw[rows, columns].astype(jnp.float32)
                target[g, rows_to, :] = (part * factor * gain[:, columns]).astype(jnp.bfloat16)
            return carry

        lax.fori_loop(0, tokens // NORM_ROWS, step, 0)

    loads[0].wait()
    loads[1].wait()
    normalise(key_raw, key_gain, key_buf, me * tokens)
    for group in range(first):
        for off in range(1, n):
            key_send(off, group).start()

    loads[2].wait()
    loads[3].wait()
    codes[me] = jnp.zeros(codes.shape[1:], jnp.int32)
    for b in range(block_count):
        used = counts[b, pl.ds(clip, 1), :]
        code = jnp.zeros((1, own_heads), jnp.int32)
        for s in range(block_count):
            named = lists[b, s, pl.ds(clip, 1), :]
            for e in range(block_count):
                code = code + jnp.where((named == e) & (used > s), 1 << e, 0)
        codes[me, pl.ds(b, 1), pl.ds(0, own_heads)] = code

    def code_message(off, source):
        return pltpu.make_async_remote_copy(
            src_ref=codes.at[source],
            dst_ref=codes.at[source],
            send_sem=code_send_sem.at[off - 1],
            recv_sem=code_recv_sem.at[off - 1],
            device_id={"seq": lax.rem(me + off, n)},
            device_id_type=MESH,
        )

    for off in range(1, n):
        code_message(off, me).start()
    loads[4].wait()
    loads[5].wait()
    normalise(query_raw, query_gain, query_buf, 0)
    for off in range(1, n):
        code_message(off, lax.rem(me + n - off, n)).wait_recv()
    code_load = pltpu.make_async_copy(codes, codes_smem, code_load_sem)
    code_load.start()
    code_load.wait()

    exponent_scale = math.log2(math.e) / math.sqrt(HD)

    def weigh(group, j):
        head = group * PAIR + j
        columns = slice(j * HD, (j + 1) * HD)
        scores = lax.dot_general(
            query_buf[group, :, columns],
            key_buf[group, :, columns],
            (((1,), (1,)), ((), ())),
            preferred_element_type=jnp.float32,
        )
        owner = head // own_heads
        own_head = head - owner * own_heads
        weights, sums = [], []
        for r in range(tokens // row_group):
            code = codes_smem[owner, (me * tokens + r * row_group) // BLK, own_head]
            pieces = []
            for e in range(block_count):
                allowed = jnp.bitwise_and(code, 1 << e) != 0
                bias = jnp.where(allowed, jnp.float32(0.0), jnp.float32(MASKED))
                pieces.append(
                    scores[r * row_group : (r + 1) * row_group, e * BLK : (e + 1) * BLK] + bias
                )
            masked = jnp.concatenate(pieces, axis=1)
            highest = jnp.max(masked, axis=-1, keepdims=True)
            weight = jnp.exp2((masked - highest) * exponent_scale)
            sums.append(jnp.sum(weight, axis=-1, keepdims=True))
            weights.append(weight.astype(jnp.bfloat16))
        return jnp.concatenate(weights, axis=0), 1.0 / jnp.concatenate(sums, axis=0)

    def gather(group, j, weight, inverse):
        numerator = jnp.dot(
            weight,
            value_buf[group, :, j * HD : (j + 1) * HD],
            preferred_element_type=jnp.float32,
        )
        columns = pl.ds(pl.multiple_of((group * PAIR + j) * HD, HD), HD)
        out_ref[0, :, columns] = (numerator * inverse).astype(jnp.bfloat16)

    def visit(group, carry):
        for off in range(1, n):
            value_send(off, group).wait_send()
            key_send(off, group).wait_send()

        @pl.when(group + AHEAD < groups)
        def _():
            for off in range(1, n):
                key_send(off, group + AHEAD).start()
            for off in range(1, n):
                value_send(off, group + AHEAD).start()

        sources = [(off, lax.rem(me + n - off, n)) for off in range(1, n)]
        for off, source in sources:
            message(key_buf, 1, off, group, source).wait_recv()
        weighed = [weigh(group, j) for j in range(PAIR)]
        value_load(group).wait()
        for off, source in sources:
            message(value_buf, 0, off, group, source).wait_recv()
        for j in range(PAIR):
            gather(group, j, *weighed[j])
        return carry

    lax.fori_loop(0, groups, visit, 0)
    for off in range(1, n):
        code_message(off, me).wait_send()


def shards(n, query_rows, key_rows, value_rows, query_gain, key_gain, tile_lists, tile_counts):
    _, tokens, width = query_rows.shape
    lists = jnp.transpose(tile_lists, (2, 3, 0, 1))
    counts = jnp.transpose(tile_counts, (2, 0, 1))
    block_count = lists.shape[0]
    group_width = PAIR * HD
    groups = width // group_width
    code_rows = -(-block_count // 8) * 8
    visited = tokens * n * tokens * width
    return pl.pallas_call(
        functools.partial(kernel, n),
        out_shape=pltpu.VMEM(query_rows.shape, jnp.bfloat16),
        in_specs=[pl.BlockSpec(memory_space=pltpu.HBM)] * 7,
        out_specs=pl.BlockSpec(memory_space=pltpu.VMEM),
        scratch_shapes=[
            pltpu.VMEM((tokens, width), jnp.bfloat16),
            pltpu.VMEM((tokens, width), jnp.bfloat16),
            pltpu.VMEM((groups, tokens, group_width), jnp.bfloat16),
            pltpu.VMEM((groups, n * tokens, group_width), jnp.bfloat16),
            pltpu.VMEM((groups, n * tokens, group_width), jnp.bfloat16),
            pltpu.VMEM((1, width), jnp.float32),
            pltpu.VMEM((1, width), jnp.float32),
            pltpu.VMEM(lists.shape, jnp.int32),
            pltpu.VMEM(counts.shape, jnp.int32),
            pltpu.VMEM((n, code_rows, 128), jnp.int32),
            pltpu.SMEM((n, code_rows, 128), jnp.int32),
            pltpu.SemaphoreType.DMA((6,)),
            pltpu.SemaphoreType.DMA((groups,)),
            pltpu.SemaphoreType.DMA((n - 1, 2, groups)),
            pltpu.SemaphoreType.DMA((n - 1, 2, groups)),
            pltpu.SemaphoreType.DMA((n - 1,)),
            pltpu.SemaphoreType.DMA((n - 1,)),
            pltpu.SemaphoreType.DMA,
        ],
        compiler_params=pltpu.CompilerParams(
            collective_id=0,
            has_side_effects=True,
            vmem_limit_bytes=VMEM_BYTES,
        ),
        cost_estimate=pl.CostEstimate(
            flops=4 * visited, bytes_accessed=8 * tokens * width, transcendentals=visited // HD
        ),
    )(
        *(
            pltpu.with_memory_space_constraint(operand, pltpu.HBM)
            for operand in (
                query_rows,
                key_rows,
                value_rows,
                query_gain.reshape(1, width),
                key_gain.reshape(1, width),
                lists,
                counts,
            )
        )
    )


def solution(mesh):
    in_specs = (
        P("clip", "seq", None),
        P("clip", "seq", None),
        P("clip", "seq", None),
        P(),
        P(),
        P(None, "seq", None, None),
        P(None, "seq", None),
    )
    out_specs = P("clip", "seq", None)
    return jax.shard_map(
        functools.partial(shards, mesh.shape["seq"]),
        mesh=mesh,
        in_specs=in_specs,
        out_specs=out_specs,
        check_vma=False,
    )
```

```python
import functools
import math

import jax
import jax.numpy as jnp
from jax import lax
from jax.experimental import pallas as pl
from jax.experimental.pallas import tpu as pltpu
from jax.sharding import PartitionSpec as P

HD = 128
BLK = 128
PAIR = 2
AHEAD = 4
NORM_ROWS = 16
MASKED = -1e30
VMEM_BYTES = 48 * 1024 * 1024
EPSILON = 1e-06

MESH = pl.DeviceIdType.MESH


def kernel(
    n,
    query_hbm,
    key_hbm,
    value_hbm,
    query_gain_hbm,
    key_gain_hbm,
    lists_hbm,
    counts_hbm,
    out_ref,
    value_far,
    query_raw,
    key_raw,
    query_buf,
    key_buf,
    value_buf,
    query_gain,
    key_gain,
    lists,
    counts,
    codes,
    codes_smem,
    load_sem,
    value_sem,
    send_sem,
    recv_sem,
    code_send_sem,
    code_recv_sem,
    code_load_sem,
    fetch_sem,
):
    tokens, width = query_raw.shape
    groups, _, group_width = key_buf.shape
    own_heads = lists.shape[3]
    block_count = lists.shape[0]
    row_group = math.gcd(tokens, BLK)
    first = min(AHEAD, groups)
    me = lax.axis_index("seq")
    clip = lax.axis_index("clip")

    def rows_of(device):
        return pl.ds(pl.multiple_of(device * tokens, row_group), tokens)

    def value_load(group):
        columns = pl.ds(pl.multiple_of(group * group_width, group_width), group_width)
        return pltpu.make_async_copy(
            value_hbm.at[0, :, columns], value_buf.at[group, rows_of(me)], value_sem.at[group]
        )

    loads = [
        pltpu.make_async_copy(source, target, load_sem.at[i])
        for i, (source, target) in enumerate(
            [
                (key_hbm.at[0], key_raw),
                (key_gain_hbm, key_gain),
                (lists_hbm, lists),
                (counts_hbm, counts),
                (query_hbm.at[0], query_raw),
                (query_gain_hbm, query_gain),
            ]
        )
    ]
    barrier = pltpu.get_barrier_semaphore()
    for off in range(1, n):
        pl.semaphore_signal(
            barrier, inc=1, device_id={"seq": lax.rem(me + off, n)}, device_id_type=MESH
        )
    for load in loads:
        load.start()
    pl.semaphore_wait(barrier, n - 1)

    def message(buf, kind, off, group, source):
        place = (group, rows_of(source))
        return pltpu.make_async_remote_copy(
            src_ref=buf.at[place],
            dst_ref=buf.at[place],
            send_sem=send_sem.at[off - 1, kind, group],
            recv_sem=recv_sem.at[off - 1, kind, group],
            device_id={"seq": lax.rem(me + off, n)},
            device_id_type=MESH,
        )

    def value_send(off, group):
        columns = pl.ds(pl.multiple_of(group * group_width, group_width), group_width)
        return pltpu.make_async_remote_copy(
            src_ref=value_hbm.at[0, :, columns],
            dst_ref=value_far.at[me, :, columns],
            send_sem=send_sem.at[off - 1, 0, group],
            recv_sem=recv_sem.at[off - 1, 0, group],
            device_id={"seq": lax.rem(me + off, n)},
            device_id_type=MESH,
        )

    def value_arrival(off, group, source):
        columns = pl.ds(pl.multiple_of(group * group_width, group_width), group_width)
        place = (source, slice(None), columns)
        return pltpu.make_async_remote_copy(
            src_ref=value_far.at[place],
            dst_ref=value_far.at[place],
            send_sem=send_sem.at[off - 1, 0, group],
            recv_sem=recv_sem.at[off - 1, 0, group],
            device_id={"seq": lax.rem(me + off, n)},
            device_id_type=MESH,
        )

    def value_fetch(off, group, source):
        columns = pl.ds(pl.multiple_of(group * group_width, group_width), group_width)
        return pltpu.make_async_copy(
            value_far.at[source, :, columns],
            value_buf.at[group, rows_of(source)],
            fetch_sem.at[off - 1, group],
        )

    def key_send(off, group):
        return message(key_buf, 1, off, group, me)

    for group in range(first):
        for off in range(1, n):
            value_send(off, group).start()

    def load_values(group, carry):
        value_load(group).start()
        return carry

    lax.fori_loop(0, groups, load_values, 0)

    def normalise(raw, gain, target, first_row):
        def step(i, carry):
            rows = pl.ds(pl.multiple_of(i * NORM_ROWS, NORM_ROWS), NORM_ROWS)
            rows_to = pl.ds(pl.multiple_of(first_row + i * NORM_ROWS, NORM_ROWS), NORM_ROWS)
            total = jnp.zeros((NORM_ROWS, group_width), jnp.float32)
            for g in range(groups):
                part = raw[rows, g * group_width : (g + 1) * group_width].astype(jnp.float32)
                total = total + part * part
            spread = jnp.sum(total, axis=-1, keepdims=True) * (1.0 / width)
            factor = lax.rsqrt(spread + EPSILON)
            for g in range(groups):
                columns = slice(g * group_width, (g + 1) * group_width)
                part = raw[rows, columns].astype(jnp.float32)
                target[g, rows_to, :] = (part * factor * gain[:, columns]).astype(jnp.bfloat16)
            return carry

        lax.fori_loop(0, tokens // NORM_ROWS, step, 0)

    loads[0].wait()
    loads[1].wait()
    normalise(key_raw, key_gain, key_buf, me * tokens)
    for group in range(first):
        for off in range(1, n):
            key_send(off, group).start()

    loads[2].wait()
    loads[3].wait()
    codes[me] = jnp.zeros(codes.shape[1:], jnp.int32)
    for b in range(block_count):
        used = counts[b, pl.ds(clip, 1), :]
        code = jnp.zeros((1, own_heads), jnp.int32)
        for s in range(block_count):
            named = lists[b, s, pl.ds(clip, 1), :]
            for e in range(block_count):
                code = code + jnp.where((named == e) & (used > s), 1 << e, 0)
        codes[me, pl.ds(b, 1), pl.ds(0, own_heads)] = code

    def code_message(off, source):
        return pltpu.make_async_remote_copy(
            src_ref=codes.at[source],
            dst_ref=codes.at[source],
            send_sem=code_send_sem.at[off - 1],
            recv_sem=code_recv_sem.at[off - 1],
            device_id={"seq": lax.rem(me + off, n)},
            device_id_type=MESH,
        )

    for off in range(1, n):
        code_message(off, me).start()
    loads[4].wait()
    loads[5].wait()
    normalise(query_raw, query_gain, query_buf, 0)
    for off in range(1, n):
        code_message(off, lax.rem(me + n - off, n)).wait_recv()
    code_load = pltpu.make_async_copy(codes, codes_smem, code_load_sem)
    code_load.start()
    code_load.wait()

    exponent_scale = math.log2(math.e) / math.sqrt(HD)

    def weigh(group, j):
        head = group * PAIR + j
        columns = slice(j * HD, (j + 1) * HD)
        scores = lax.dot_general(
            query_buf[group, :, columns],
            key_buf[group, :, columns],
            (((1,), (1,)), ((), ())),
            preferred_element_type=jnp.float32,
        )
        owner = head // own_heads
        own_head = head - owner * own_heads
        weights, sums = [], []
        for r in range(tokens // row_group):
            code = codes_smem[owner, (me * tokens + r * row_group) // BLK, own_head]
            pieces = []
            for e in range(block_count):
                allowed = jnp.bitwise_and(code, 1 << e) != 0
                bias = jnp.where(allowed, jnp.float32(0.0), jnp.float32(MASKED))
                pieces.append(
                    scores[r * row_group : (r + 1) * row_group, e * BLK : (e + 1) * BLK] + bias
                )
            masked = jnp.concatenate(pieces, axis=1)
            highest = jnp.max(masked, axis=-1, keepdims=True)
            weight = jnp.exp2((masked - highest) * exponent_scale)
            sums.append(jnp.sum(weight, axis=-1, keepdims=True))
            weights.append(weight.astype(jnp.bfloat16))
        return jnp.concatenate(weights, axis=0), 1.0 / jnp.concatenate(sums, axis=0)

    def gather(group, j, weight, inverse):
        numerator = jnp.dot(
            weight,
            value_buf[group, :, j * HD : (j + 1) * HD],
            preferred_element_type=jnp.float32,
        )
        columns = pl.ds(pl.multiple_of((group * PAIR + j) * HD, HD), HD)
        out_ref[0, :, columns] = (numerator * inverse).astype(jnp.bfloat16)

    def visit(group, carry):
        for off in range(1, n):
            value_send(off, group).wait_send()
            key_send(off, group).wait_send()

        @pl.when(group + AHEAD < groups)
        def _():
            for off in range(1, n):
                key_send(off, group + AHEAD).start()
            for off in range(1, n):
                value_send(off, group + AHEAD).start()

        sources = [(off, lax.rem(me + n - off, n)) for off in range(1, n)]
        for off, source in sources:
            message(key_buf, 1, off, group, source).wait_recv()
        weighed = [weigh(group, j) for j in range(PAIR)]
        value_load(group).wait()
        for off, source in sources:
            value_arrival(off, group, source).wait_recv()
            value_fetch(off, group, source).start()
        for off, source in sources:
            value_fetch(off, group, source).wait()
        for j in range(PAIR):
            gather(group, j, *weighed[j])
        return carry

    lax.fori_loop(0, groups, visit, 0)
    for off in range(1, n):
        code_message(off, me).wait_send()


def shards(n, query_rows, key_rows, value_rows, query_gain, key_gain, tile_lists, tile_counts):
    _, tokens, width = query_rows.shape
    lists = jnp.transpose(tile_lists, (2, 3, 0, 1))
    counts = jnp.transpose(tile_counts, (2, 0, 1))
    block_count = lists.shape[0]
    group_width = PAIR * HD
    groups = width // group_width
    code_rows = -(-block_count // 8) * 8
    visited = tokens * n * tokens * width
    attended, _ = pl.pallas_call(
        functools.partial(kernel, n),
        out_shape=(
            pltpu.VMEM(query_rows.shape, jnp.bfloat16),
            pltpu.HBM((n, tokens, width), jnp.bfloat16),
        ),
        in_specs=[pl.BlockSpec(memory_space=pltpu.HBM)] * 7,
        out_specs=(
            pl.BlockSpec(memory_space=pltpu.VMEM),
            pl.BlockSpec(memory_space=pltpu.HBM),
        ),
        scratch_shapes=[
            pltpu.VMEM((tokens, width), jnp.bfloat16),
            pltpu.VMEM((tokens, width), jnp.bfloat16),
            pltpu.VMEM((groups, tokens, group_width), jnp.bfloat16),
            pltpu.VMEM((groups, n * tokens, group_width), jnp.bfloat16),
            pltpu.VMEM((groups, n * tokens, group_width), jnp.bfloat16),
            pltpu.VMEM((1, width), jnp.float32),
            pltpu.VMEM((1, width), jnp.float32),
            pltpu.VMEM(lists.shape, jnp.int32),
            pltpu.VMEM(counts.shape, jnp.int32),
            pltpu.VMEM((n, code_rows, 128), jnp.int32),
            pltpu.SMEM((n, code_rows, 128), jnp.int32),
            pltpu.SemaphoreType.DMA((6,)),
            pltpu.SemaphoreType.DMA((groups,)),
            pltpu.SemaphoreType.DMA((n - 1, 2, groups)),
            pltpu.SemaphoreType.DMA((n - 1, 2, groups)),
            pltpu.SemaphoreType.DMA((n - 1,)),
            pltpu.SemaphoreType.DMA((n - 1,)),
            pltpu.SemaphoreType.DMA,
            pltpu.SemaphoreType.DMA((n - 1, groups)),
        ],
        compiler_params=pltpu.CompilerParams(
            collective_id=0,
            has_side_effects=True,
            vmem_limit_bytes=VMEM_BYTES,
        ),
        cost_estimate=pl.CostEstimate(
            flops=4 * visited, bytes_accessed=8 * tokens * width, transcendentals=visited // HD
        ),
    )(
        *(
            pltpu.with_memory_space_constraint(operand, pltpu.HBM)
            for operand in (
                query_rows,
                key_rows,
                value_rows,
                query_gain.reshape(1, width),
                key_gain.reshape(1, width),
                lists,
                counts,
            )
        )
    )
    return attended


def solution(mesh):
    in_specs = (
        P("clip", "seq", None),
        P("clip", "seq", None),
        P("clip", "seq", None),
        P(),
        P(),
        P(None, "seq", None, None),
        P(None, "seq", None),
    )
    out_specs = P("clip", "seq", None)
    return jax.shard_map(
        functools.partial(shards, mesh.shape["seq"]),
        mesh=mesh,
        in_specs=in_specs,
        out_specs=out_specs,
        check_vma=False,
    )
```

```python
import functools
import math

import jax
import jax.numpy as jnp
from jax import lax
from jax.experimental import pallas as pl
from jax.experimental.pallas import tpu as pltpu
from jax.sharding import PartitionSpec as P

HD = 128
BLK = 128
PAIR = 4
AHEAD = 3
NORM_ROWS = 16
MASKED = -1e30
OUT_ROWS = 48
VMEM_BYTES = 48 * 1024 * 1024
EPSILON = 1e-06

MESH = pl.DeviceIdType.MESH


def kernel(
    n,
    query_hbm,
    key_hbm,
    value_hbm,
    query_gain_hbm,
    key_gain_hbm,
    lists_hbm,
    counts_hbm,
    out_ref,
    query_raw,
    key_raw,
    query_buf,
    key_buf,
    value_buf,
    query_gain,
    key_gain,
    lists,
    counts,
    codes,
    codes_smem,
    load_sem,
    value_sem,
    send_sem,
    recv_sem,
    code_send_sem,
    code_recv_sem,
    code_load_sem,
):
    tokens, width = query_raw.shape
    groups, _, group_width = key_buf.shape
    own_heads = lists.shape[3]
    block_count = lists.shape[0]
    row_group = math.gcd(tokens, BLK)
    first = min(AHEAD, groups)
    me = lax.axis_index("seq")
    clip = lax.axis_index("clip")

    def rows_of(device):
        return pl.ds(pl.multiple_of(device * tokens, row_group), tokens)

    def value_load(group):
        columns = pl.ds(pl.multiple_of(group * group_width, group_width), group_width)
        return pltpu.make_async_copy(
            value_hbm.at[0, :, columns], value_buf.at[group, rows_of(me)], value_sem.at[group]
        )

    loads = [
        pltpu.make_async_copy(source, target, load_sem.at[i])
        for i, (source, target) in enumerate(
            [
                (key_hbm.at[0], key_raw),
                (key_gain_hbm, key_gain),
                (lists_hbm, lists),
                (counts_hbm, counts),
                (query_hbm.at[0], query_raw),
                (query_gain_hbm, query_gain),
            ]
        )
    ]
    barrier = pltpu.get_barrier_semaphore()
    for off in range(1, n):
        pl.semaphore_signal(
            barrier, inc=1, device_id={"seq": lax.rem(me + off, n)}, device_id_type=MESH
        )
    for load in loads:
        load.start()
    pl.semaphore_wait(barrier, n - 1)

    def message(buf, kind, off, group, source):
        place = (group, rows_of(source))
        return pltpu.make_async_remote_copy(
            src_ref=buf.at[place],
            dst_ref=buf.at[place],
            send_sem=send_sem.at[off - 1, kind, group],
            recv_sem=recv_sem.at[off - 1, kind, group],
            device_id={"seq": lax.rem(me + off, n)},
            device_id_type=MESH,
        )

    def value_send(off, group):
        columns = pl.ds(pl.multiple_of(group * group_width, group_width), group_width)
        return pltpu.make_async_remote_copy(
            src_ref=value_hbm.at[0, :, columns],
            dst_ref=value_buf.at[group, rows_of(me)],
            send_sem=send_sem.at[off - 1, 0, group],
            recv_sem=recv_sem.at[off - 1, 0, group],
            device_id={"seq": lax.rem(me + off, n)},
            device_id_type=MESH,
        )

    def key_send(off, group):
        return message(key_buf, 1, off, group, me)

    for group in range(first):
        for off in range(1, n):
            value_send(off, group).start()

    def load_values(group, carry):
        value_load(group).start()
        return carry

    lax.fori_loop(0, groups, load_values, 0)

    def normalise(raw, gain, target, first_row):
        def step(i, carry):
            rows = pl.ds(pl.multiple_of(i * NORM_ROWS, NORM_ROWS), NORM_ROWS)
            rows_to = pl.ds(pl.multiple_of(first_row + i * NORM_ROWS, NORM_ROWS), NORM_ROWS)
            total = jnp.zeros((NORM_ROWS, group_width), jnp.float32)
            for g in range(groups):
                part = raw[rows, g * group_width : (g + 1) * group_width].astype(jnp.float32)
                total = total + part * part
            spread = jnp.sum(total, axis=-1, keepdims=True) * (1.0 / width)
            factor = lax.rsqrt(spread + EPSILON)
            for g in range(groups):
                columns = slice(g * group_width, (g + 1) * group_width)
                part = raw[rows, columns].astype(jnp.float32)
                target[g, rows_to, :] = (part * factor * gain[:, columns]).astype(jnp.bfloat16)
            return carry

        lax.fori_loop(0, tokens // NORM_ROWS, step, 0)

    loads[0].wait()
    loads[1].wait()
    normalise(key_raw, key_gain, key_buf, me * tokens)
    for group in range(first):
        for off in range(1, n):
            key_send(off, group).start()

    loads[2].wait()
    loads[3].wait()
    codes[me] = jnp.zeros(codes.shape[1:], jnp.int32)
    for b in range(block_count):
        used = counts[b, pl.ds(clip, 1), :]
        code = jnp.zeros((1, own_heads), jnp.int32)
        for s in range(block_count):
            named = lists[b, s, pl.ds(clip, 1), :]
            for e in range(block_count):
                code = code + jnp.where((named == e) & (used > s), 1 << e, 0)
        codes[me, pl.ds(b, 1), pl.ds(0, own_heads)] = code

    def code_message(off, source):
        return pltpu.make_async_remote_copy(
            src_ref=codes.at[source],
            dst_ref=codes.at[source],
            send_sem=code_send_sem.at[off - 1],
            recv_sem=code_recv_sem.at[off - 1],
            device_id={"seq": lax.rem(me + off, n)},
            device_id_type=MESH,
        )

    for off in range(1, n):
        code_message(off, me).start()
    loads[4].wait()
    loads[5].wait()
    normalise(query_raw, query_gain, query_buf, 0)
    for off in range(1, n):
        code_message(off, lax.rem(me + n - off, n)).wait_recv()
    code_load = pltpu.make_async_copy(codes, codes_smem, code_load_sem)
    code_load.start()
    code_load.wait()

    exponent_scale = math.log2(math.e) / math.sqrt(HD)

    def weigh(group, j):
        head = group * PAIR + j
        columns = slice(j * HD, (j + 1) * HD)
        scores = lax.dot_general(
            query_buf[group, :, columns],
            key_buf[group, :, columns],
            (((1,), (1,)), ((), ())),
            preferred_element_type=jnp.float32,
        )
        owner = head // own_heads
        own_head = head - owner * own_heads
        weights, sums = [], []
        for r in range(tokens // row_group):
            code = codes_smem[owner, (me * tokens + r * row_group) // BLK, own_head]
            pieces = []
            for e in range(block_count):
                allowed = jnp.bitwise_and(code, 1 << e) != 0
                bias = jnp.where(allowed, jnp.float32(0.0), jnp.float32(MASKED))
                pieces.append(
                    scores[r * row_group : (r + 1) * row_group, e * BLK : (e + 1) * BLK] + bias
                )
            masked = jnp.concatenate(pieces, axis=1)
            highest = jnp.max(masked, axis=-1, keepdims=True)
            weight = jnp.exp2((masked - highest) * exponent_scale)
            sums.append(jnp.sum(weight, axis=-1, keepdims=True))
            weights.append(weight.astype(jnp.bfloat16))
        return jnp.concatenate(weights, axis=0), 1.0 / jnp.concatenate(sums, axis=0)

    def gather(group, j, weight, inverse):
        numerator = jnp.dot(
            weight,
            value_buf[group, :, j * HD : (j + 1) * HD],
            preferred_element_type=jnp.float32,
        )
        columns = pl.ds(pl.multiple_of((group * PAIR + j) * HD, HD), HD)
        out_ref[0, :, columns] = (numerator * inverse).astype(jnp.bfloat16)

    def visit(group, carry):
        for off in range(1, n):
            value_send(off, group).wait_send()
            key_send(off, group).wait_send()

        @pl.when(group + AHEAD < groups)
        def _():
            for off in range(1, n):
                key_send(off, group + AHEAD).start()
            for off in range(1, n):
                value_send(off, group + AHEAD).start()

        sources = [(off, lax.rem(me + n - off, n)) for off in range(1, n)]
        for off, source in sources:
            message(key_buf, 1, off, group, source).wait_recv()
        weighed = [weigh(group, j) for j in range(PAIR)]
        value_load(group).wait()
        for off, source in sources:
            message(value_buf, 0, off, group, source).wait_recv()
        for j in range(PAIR):
            gather(group, j, *weighed[j])
        return carry

    lax.fori_loop(0, groups, visit, 0)
    for off in range(1, n):
        code_message(off, me).wait_send()


def write_out(rows, held, out_hbm, sem):
    pieces = [
        pltpu.make_async_copy(
            held.at[0, pl.ds(i * rows, rows)], out_hbm.at[0, pl.ds(i * rows, rows)], sem.at[i]
        )
        for i in range(held.shape[1] // rows)
    ]
    for piece in pieces:
        piece.start()
    for piece in pieces:
        piece.wait()


def shards(n, query_rows, key_rows, value_rows, query_gain, key_gain, tile_lists, tile_counts):
    _, tokens, width = query_rows.shape
    lists = jnp.transpose(tile_lists, (2, 3, 0, 1))
    counts = jnp.transpose(tile_counts, (2, 0, 1))
    block_count = lists.shape[0]
    group_width = PAIR * HD
    groups = width // group_width
    code_rows = -(-block_count // 8) * 8
    visited = tokens * n * tokens * width
    attended = pl.pallas_call(
        functools.partial(kernel, n),
        out_shape=pltpu.VMEM(query_rows.shape, jnp.bfloat16),
        in_specs=[pl.BlockSpec(memory_space=pltpu.HBM)] * 7,
        out_specs=pl.BlockSpec(memory_space=pltpu.VMEM),
        scratch_shapes=[
            pltpu.VMEM((tokens, width), jnp.bfloat16),
            pltpu.VMEM((tokens, width), jnp.bfloat16),
            pltpu.VMEM((groups, tokens, group_width), jnp.bfloat16),
            pltpu.VMEM((groups, n * tokens, group_width), jnp.bfloat16),
            pltpu.VMEM((groups, n * tokens, group_width), jnp.bfloat16),
            pltpu.VMEM((1, width), jnp.float32),
            pltpu.VMEM((1, width), jnp.float32),
            pltpu.VMEM(lists.shape, jnp.int32),
            pltpu.VMEM(counts.shape, jnp.int32),
            pltpu.VMEM((n, code_rows, 128), jnp.int32),
            pltpu.SMEM((n, code_rows, 128), jnp.int32),
            pltpu.SemaphoreType.DMA((6,)),
            pltpu.SemaphoreType.DMA((groups,)),
            pltpu.SemaphoreType.DMA((n - 1, 2, groups)),
            pltpu.SemaphoreType.DMA((n - 1, 2, groups)),
            pltpu.SemaphoreType.DMA((n - 1,)),
            pltpu.SemaphoreType.DMA((n - 1,)),
            pltpu.SemaphoreType.DMA,
        ],
        compiler_params=pltpu.CompilerParams(
            collective_id=0,
            has_side_effects=True,
            vmem_limit_bytes=VMEM_BYTES,
        ),
        cost_estimate=pl.CostEstimate(
            flops=4 * visited, bytes_accessed=8 * tokens * width, transcendentals=visited // HD
        ),
    )(
        *(
            pltpu.with_memory_space_constraint(operand, pltpu.HBM)
            for operand in (
                query_rows,
                key_rows,
                value_rows,
                query_gain.reshape(1, width),
                key_gain.reshape(1, width),
                lists,
                counts,
            )
        )
    )
    rows = math.gcd(tokens, OUT_ROWS)
    return pl.pallas_call(
        functools.partial(write_out, rows),
        out_shape=jax.ShapeDtypeStruct(query_rows.shape, jnp.bfloat16),
        in_specs=[pl.BlockSpec(memory_space=pltpu.VMEM)],
        out_specs=pl.BlockSpec(memory_space=pltpu.HBM),
        scratch_shapes=[pltpu.SemaphoreType.DMA((tokens // rows,))],
        cost_estimate=pl.CostEstimate(
            flops=0, bytes_accessed=4 * tokens * width, transcendentals=0
        ),
    )(attended)


def solution(mesh):
    in_specs = (
        P("clip", "seq", None),
        P("clip", "seq", None),
        P("clip", "seq", None),
        P(),
        P(),
        P(None, "seq", None, None),
        P(None, "seq", None),
    )
    out_specs = P("clip", "seq", None)
    return jax.shard_map(
        functools.partial(shards, mesh.shape["seq"]),
        mesh=mesh,
        in_specs=in_specs,
        out_specs=out_specs,
        check_vma=False,
    )
```
